256 devices in a mesh: cuts: 4 (over z_hi), fsdp: 32 (over x, y, core), dp: 2 (over z_lo).
Axes of the slice: x: 4, y: 4, z: 8 (z_hi: 4, z_lo: 2; z = z_hi * 2 + z_lo), core: 2. Of those that a mesh axis runs over, the one named last changes fastest.
Arguments:
- grads: float32 [256, 1048576], P(('cuts', 'fsdp', 'dp')), may hold values from -0.9765625 to 0.9765625, as said below
- residual: float32 [4, 1048576], P('cuts', ('fsdp', 'dp')), may hold values from -0.125 to 0.125, as said below
- master: float32 [1048576], P(('fsdp', 'dp')), may hold values from -6 to 6
- moment_one: float32 [1048576], P(('fsdp', 'dp')), may hold values from -6 to 6
- moment_two: float32 [1048576], P(('fsdp', 'dp')), may hold values from 0.1 to 10
Outputs:
- params: bfloat16 [1048576], replicated
- new_master: float32 [1048576], P(('fsdp', 'dp'))
- new_moment_one: float32 [1048576], P(('fsdp', 'dp'))
- new_moment_two: float32 [1048576], P(('fsdp', 'dp'))
- new_residual: float32 [4, 1048576], P('cuts', ('fsdp', 'dp'))
The draws below stay inside these ranges and needn't reach their ends.
Inputs may be any that keep to these rules, and one draw needn't show every extreme that they name: `grads`: every entry is a whole multiple of 2^-8. `residual`: every entry is a whole multiple of 2^-12.
All inputs are finite; a program needn't handle non-finite values.
Results may differ from the reference program's by a relative error of at most 0.015.
Values may be sent and summed in bfloat16 or wider, within the bound.
No kernel may reach another device: no remote copies, remote signals or barrier semaphores. Data moves between devices by JAX's collectives and lax.ppermute only.
A program may use at most 64 MiB of HBM per device.

```python
import math
import jax
import jax.numpy as jnp
from jax import lax

STEP = 10
BUCKET = 1048576
N_CUTS = 4
N_FSDP = 32
N_DP = 2
DEVICES = 256


def draw_grads(key, part):
    key = jax.random.fold_in(key, 11)
    own_key = jax.random.fold_in(key, 1)
    units = jax.random.randint(own_key, (DEVICES, BUCKET), -250, 251).astype(jnp.float32)
    return units * (1.0 / 256.0)


def draw_residual(key, part):
    key = jax.random.fold_in(key, 23)
    units = jax.random.randint(key, (N_CUTS, BUCKET), -512, 513).astype(jnp.float32)
    return units * (1.0 / 4096.0)


def shard_levels(stream_key, shape, shards, least, high):
    factor_of, own = 1.0, jax.random.fold_in(stream_key, 6)
    for dim, blocks in shards:
        heights = jnp.exp(jax.random.uniform(jax.random.fold_in(own, dim), (blocks,), jnp.float32, least / len(shards), high / len(shards)))
        factor_of = factor_of * jnp.repeat(heights, shape[dim] // blocks).reshape([-1 if axis == dim else 1 for axis in range(len(shape))])
    return factor_of


def scatter_about(key, dims, deviation, limit, split=(), kind=jnp.bfloat16):
    loudness = shard_levels(key, dims, split, -0.22, 0.18) if split else 1.0
    drawn = jax.random.normal(key, dims, jnp.float32) * deviation * loudness
    return jnp.minimum(jnp.maximum(drawn, -limit), limit).astype(kind)


def setup_inputs(seed: int = 0) -> dict:
    seeds = jax.random.split(jax.random.key(seed), 6)
    grads = draw_grads(jax.random.fold_in(seeds[5], 71), 0)
    residual = draw_residual(jax.random.fold_in(seeds[5], 71), 0)
    master = scatter_about(seeds[2], (BUCKET,), 0.5, 6.0, ((0, 64),), jnp.float32)
    moment_one = scatter_about(seeds[3], (BUCKET,), 1.0, 6.0, ((0, 64),), jnp.float32)
    moment_two = jnp.clip(jnp.exp(math.log(10.0) - 4.6051702 * jax.random.uniform(seeds[4], (BUCKET,), jnp.float32) ** shard_levels(seeds[4], (BUCKET,), ((0, 64),), -0.2, 0.2)), 0.1, 10.0)
    return dict(grads=grads, residual=residual, master=master, moment_one=moment_one, moment_two=moment_two)


def reference(grads, residual, master, moment_one, moment_two):
    grouped = grads.reshape(N_CUTS, N_FSDP * N_DP, BUCKET)
    slice_sum = lax.optimization_barrier(jnp.sum(grouped, axis=1, dtype=jnp.float32))
    corrected = slice_sum + residual
    sent = jnp.floor(corrected * 4.0 + 0.5) * 0.25
    new_residual = corrected - sent
    gradient = lax.optimization_barrier(jnp.sum(sent, axis=0))
    new_moment_one = 0.9 * moment_one + 0.1 * gradient
    new_moment_two = 0.95 * moment_two + 0.05 * gradient * gradient
    first_hat = new_moment_one / (1.0 - 0.9 ** STEP)
    second_hat = new_moment_two / (1.0 - 0.95 ** STEP)
    new_master = master - 0.003 * (first_hat / (jnp.sqrt(second_hat) + 1e-08) + 0.1 * master)
    params = new_master.astype(jnp.bfloat16)
    return (params, new_master, new_moment_one, new_moment_two, new_residual)
```

```python
import jax
import jax.numpy as jnp
from jax import lax
from jax.experimental import pallas as pl
from jax.experimental.pallas import tpu as pltpu
from jax.sharding import Mesh, PartitionSpec as P

STEP = 10
OWN = ("x", "y", "core", "dp")
CHIPS = ("x", "y", "dp")
TILE = (128, 128)
ROWS = 4


def narrow_kernel(core_ref, grads_ref, out_ref):
    out_ref[...] = grads_ref[:, 0].astype(jnp.bfloat16)


def narrow_other(core, grads):
    return pl.pallas_call(
        narrow_kernel,
        grid_spec=pltpu.PrefetchScalarGridSpec(
            num_scalar_prefetch=1,
            grid=(16 // ROWS,),
            in_specs=[pl.BlockSpec((ROWS, 1, 2, *TILE), lambda i, core: (i, 1 - core[0], 0, 0, 0))],
            out_specs=pl.BlockSpec((ROWS, 2, *TILE), lambda i, core: (i, 0, 0, 0)),
        ),
        out_shape=jax.ShapeDtypeStruct((16, 2, *TILE), jnp.bfloat16),
        name="narrow_other",
    )(core, grads)


def pair_kernel(core_ref, grads_ref, other_ref, out_ref):
    total = grads_ref[:, 0] + other_ref[...].astype(jnp.float32)
    inner = jnp.clip(total, -1.0, 1.0)
    out_ref[...] = jnp.where(total == inner, total, (total - inner) * 1024.0).astype(jnp.bfloat16)


def pair_sum(core, grads, other):
    return pl.pallas_call(
        pair_kernel,
        grid_spec=pltpu.PrefetchScalarGridSpec(
            num_scalar_prefetch=1,
            grid=(16 // ROWS,),
            in_specs=[
                pl.BlockSpec((ROWS, 1, 2, *TILE), lambda i, core: (i, core[0], 0, 0, 0)),
                pl.BlockSpec((ROWS, 2, *TILE), lambda i, core: (i, 0, 0, 0)),
            ],
            out_specs=pl.BlockSpec((ROWS, 2, *TILE), lambda i, core: (i, 0, 0, 0)),
        ),
        out_shape=jax.ShapeDtypeStruct((16, 2, *TILE), jnp.bfloat16),
        name="pair_sum",
    )(core, grads, other)


def decoded(code):
    code = code.astype(jnp.float32)
    return jnp.where(jnp.abs(code) > 2.0, code * (1.0 / 1024.0) + jnp.clip(code, -1.0, 1.0), code)


def on_device(grads, residual, master, moment_one, moment_two):
    core = lax.axis_index("core").reshape(1)
    swap = [(0, 1), (1, 0)]
    blocks = grads.reshape(16, 2, 2, *TILE)
    other = lax.ppermute(narrow_other(core, blocks), "core", swap)
    outgoing = pair_sum(core, blocks, other).reshape(32, *TILE)
    arrived = lax.all_to_all(outgoing, CHIPS, 0, 0, tiled=True)
    slice_sum = jnp.sum(decoded(arrived), axis=0)
    corrected = slice_sum + residual.reshape(TILE)
    sent = jnp.floor(corrected * 4.0 + 0.5) * 0.25
    new_residual = (corrected - sent).reshape(1, 16384)
    narrow = sent.astype(jnp.bfloat16)
    gradient = sent
    for shift in (1, 2, 3):
        gradient += lax.ppermute(narrow, "cuts", [(i, (i + shift) % 4) for i in range(4)]).astype(jnp.float32)
    master = master.reshape(TILE)
    new_moment_one = 0.9 * moment_one.reshape(TILE) + 0.1 * gradient
    new_moment_two = 0.95 * moment_two.reshape(TILE) + 0.05 * gradient * gradient
    first_hat = new_moment_one / (1.0 - 0.9**STEP)
    second_hat = new_moment_two / (1.0 - 0.95**STEP)
    new_master = master - 0.003 * (first_hat / (jnp.sqrt(second_hat) + 1e-08) + 0.1 * master)
    rounded = new_master.astype(jnp.bfloat16)
    mine = lax.all_to_all(jnp.broadcast_to(rounded, (32, *TILE)), CHIPS, 0, 0, tiled=True)
    theirs = lax.ppermute(mine, "core", swap)
    mine, theirs = mine.reshape(16, 2, *TILE), theirs.reshape(16, 2, *TILE)
    first = core[0] == 0
    params = jnp.stack([jnp.where(first, mine, theirs), jnp.where(first, theirs, mine)], axis=1)
    return (params.reshape(-1), new_master.reshape(-1), new_moment_one.reshape(-1), new_moment_two.reshape(-1), new_residual)


def solution(mesh):
    mesh = Mesh(mesh.devices.reshape(4, 4, 4, 2, 2), ("cuts",) + OWN)
    own = P(OWN)
    return jax.shard_map(
        on_device,
        mesh=mesh,
        in_specs=(P(("cuts",) + OWN, None), P("cuts", OWN), own, own, own),
        out_specs=(P(), own, own, own, P("cuts", OWN)),
        check_vma=False,
    )
```

```python
import jax
import jax.numpy as jnp
from jax import lax
from jax.sharding import Mesh, PartitionSpec as P

STEP = 10
OWN = ("x", "y", "core", "dp")
CHIPS = ("x", "y", "dp")
TILE = (128, 128)
SWAP = [(0, 1), (1, 0)]


def coded(total):
    inner = jnp.clip(total, -1.0, 1.0)
    return jnp.where(total == inner, total, (total - inner) * 1024.0).astype(jnp.bfloat16)


def decoded(code):
    code = code.astype(jnp.float32)
    return jnp.where(jnp.abs(code) > 2.0, code * (1.0 / 1024.0) + jnp.clip(code, -1.0, 1.0), code)


def on_device(grads, residual, master, moment_one, moment_two):
    core = lax.axis_index("core")
    blocks = lax.optimization_barrier(grads.reshape(16, 2, 2, *TILE))
    half = lambda blocks, which: lax.dynamic_index_in_dim(blocks, which, 1, False).astype(jnp.bfloat16)
    leaving = half(blocks, 1 - core)
    other = lax.ppermute(leaving, "core", SWAP)
    blocks, _ = lax.optimization_barrier((blocks, leaving))
    own = lax.optimization_barrier(half(blocks, core))
    total = own.astype(jnp.float32) + other.astype(jnp.float32)
    arrived = lax.all_to_all(coded(total).reshape(32, *TILE), CHIPS, 0, 0, tiled=True)
    slice_sum = jnp.sum(decoded(arrived), axis=0).reshape(-1)
    corrected = slice_sum + residual[0]
    sent = jnp.floor(corrected * 4.0 + 0.5) * 0.25
    new_residual = (corrected - sent)[None]
    narrow = sent.astype(jnp.bfloat16)
    sents = [lax.ppermute(narrow, "cuts", [(i, (i + shift) % 4) for i in range(4)]) for shift in (1, 2, 3)]
    new_residual, sents = lax.optimization_barrier((new_residual, sents))
    gradient = sent + sum(one.astype(jnp.float32) for one in sents)
    new_moment_one = 0.9 * moment_one + 0.1 * gradient
    new_moment_two = 0.95 * moment_two + 0.05 * gradient * gradient
    first_hat = new_moment_one / (1.0 - 0.9**STEP)
    second_hat = new_moment_two / (1.0 - 0.95**STEP)
    new_master = master - 0.003 * (first_hat / (jnp.sqrt(second_hat) + 1e-08) + 0.1 * master)
    rounded = new_master.astype(jnp.bfloat16).reshape(TILE)
    mine = lax.all_to_all(jnp.broadcast_to(rounded, (32, *TILE)), CHIPS, 0, 0, tiled=True)
    theirs = lax.ppermute(mine, "core", SWAP)
    place = lax.broadcasted_iota(jnp.int32, (1, 2, 1, 1, 1), 1)
    params = jnp.where(place == core, mine.reshape(16, 1, 2, *TILE), theirs.reshape(16, 1, 2, *TILE))
    return (params.reshape(-1), new_master, new_moment_one, new_moment_two, new_residual)


def solution(mesh):
    mesh = Mesh(mesh.devices.reshape(4, 4, 4, 2, 2), ("cuts",) + OWN)
    own = P(OWN)
    return jax.shard_map(
        on_device,
        mesh=mesh,
        in_specs=(P(("cuts",) + OWN, None), P("cuts", OWN), own, own, own),
        out_specs=(P(), own, own, own, P("cuts", OWN)),
        check_vma=False,
    )
```

```python
import itertools

import jax
import jax.numpy as jnp
from jax import lax
from jax.sharding import Mesh, PartitionSpec as P

STEP = 10
OWN = ("x", "y", "core", "dp")
TILE = (128, 128)
SWAP = [(0, 1), (1, 0)]


def coded(total):
    inner = jnp.clip(total, -1.0, 1.0)
    return jnp.where(total == inner, total, (total - inner) * 1024.0).astype(jnp.bfloat16)


def decoded(code):
    code = code.astype(jnp.float32)
    return jnp.where(jnp.abs(code) > 2.0, code * (1.0 / 1024.0) + jnp.clip(code, -1.0, 1.0), code)


REDUCE = [(x, y, z) for z, x, y in itertools.product(range(2), range(4), range(4))]
GATHER = [(x, y, z) for z, x, y in itertools.product(range(2), range(4), range(4))]


def exchange(blocks, chips):
    groups = [
        [(((cut * 4 + x) * 4 + y) * 2 + core) * 2 + z for x, y, z in (chips[::-1] if core else chips)]
        for cut in range(4)
        for core in range(2)
    ]
    return lax.all_to_all(blocks, ("cuts",) + OWN, 0, 0, axis_index_groups=groups, tiled=True)


def outgoing(own, other, core):
    code = coded(own.astype(jnp.float32) + other.astype(jnp.float32)).reshape(4, 4, 2, *TILE)
    code = code.transpose(2, 0, 1, 3, 4)
    return (jnp.flip(code, (0, 1, 2)) if core else code).reshape(32, *TILE)


def in_place(first, second):
    first, second = first.reshape(2, 4, 4, *TILE), jnp.flip(second.reshape(2, 4, 4, *TILE), (0, 1, 2))
    first, second = (half.transpose(1, 2, 0, 3, 4).reshape(16, 2, *TILE) for half in (first, second))
    return jnp.stack([first, second], axis=1)


def on_device(grads, residual, master, moment_one, moment_two):
    core = lax.axis_index("core")
    blocks = lax.optimization_barrier(grads.reshape(16, 2, 2, *TILE))
    half = lambda blocks, which: lax.dynamic_index_in_dim(blocks, which, 1, False).astype(jnp.bfloat16)
    leaving = half(blocks, 1 - core)
    other = lax.ppermute(leaving, "core", SWAP)
    blocks, _ = lax.optimization_barrier((blocks, leaving))
    own = lax.optimization_barrier(half(blocks, core))
    zero = core == 0
    leaving = lax.cond(zero, lambda *halves: outgoing(*halves, 0), lambda *halves: outgoing(*halves, 1), own, other)
    arrived = exchange(leaving, REDUCE)
    slice_sum = jnp.sum(decoded(arrived), axis=0).reshape(-1)
    corrected = slice_sum + residual[0]
    sent = jnp.floor(corrected * 4.0 + 0.5) * 0.25
    new_residual = (corrected - sent)[None]
    narrow = sent.astype(jnp.bfloat16)
    sents = [lax.ppermute(narrow, "cuts", [(i, (i + shift) % 4) for i in range(4)]) for shift in (3, 2, 1)]
    new_residual, sents = lax.optimization_barrier((new_residual, sents))
    gradient = sent + sum(one.astype(jnp.float32) for one in sents)
    new_moment_one = 0.9 * moment_one + 0.1 * gradient
    new_moment_two = 0.95 * moment_two + 0.05 * gradient * gradient
    first_hat = new_moment_one / (1.0 - 0.9**STEP)
    second_hat = new_moment_two / (1.0 - 0.95**STEP)
    new_master = master - 0.003 * (first_hat / (jnp.sqrt(second_hat) + 1e-08) + 0.1 * master)
    rounded = new_master.astype(jnp.bfloat16).reshape(TILE)
    mine = exchange(jnp.broadcast_to(rounded, (32, *TILE)), GATHER)
    theirs = lax.ppermute(mine, "core", SWAP)
    params = in_place(jnp.where(zero, mine, theirs), jnp.where(zero, theirs, mine))
    return (params.reshape(-1), new_master, new_moment_one, new_moment_two, new_residual)


def solution(mesh):
    mesh = Mesh(mesh.devices.reshape(4, 4, 4, 2, 2), ("cuts",) + OWN)
    own = P(OWN)
    return jax.shard_map(
        on_device,
        mesh=mesh,
        in_specs=(P(("cuts",) + OWN, None), P("cuts", OWN), own, own, own),
        out_specs=(P(), own, own, own, P("cuts", OWN)),
        check_vma=False,
    )
```

```python
import itertools

import jax
import jax.numpy as jnp
from jax import lax
from jax.sharding import Mesh, PartitionSpec as P

STEP = 10
OWN = ("x", "y", "core", "dp")
TILE = (128, 128)
SWAP = [(0, 1), (1, 0)]


def coded(total):
    inner = jnp.clip(total, -1.0, 1.0)
    return jnp.where(total == inner, total, (total - inner) * 1024.0).astype(jnp.bfloat16)


def decoded(code):
    code = code.astype(jnp.float32)
    return jnp.where(jnp.abs(code) > 2.0, code * (1.0 / 1024.0) + jnp.clip(code, -1.0, 1.0), code)


REDUCE = [(x, y, z) for z, y, x in itertools.product(range(2), range(4), range(4))]
GATHER = [(x, y, z) for z, y, x in itertools.product(range(2), range(4), range(4))]


def exchange(blocks, chips):
    groups = [
        [(((cut * 4 + x) * 4 + y) * 2 + core) * 2 + z for x, y, z in (chips[::-1] if core else chips)]
        for cut in range(4)
        for core in range(2)
    ]
    return lax.all_to_all(blocks, ("cuts",) + OWN, 0, 0, axis_index_groups=groups, tiled=True)


def outgoing(own, other, core):
    code = coded(own.astype(jnp.float32) + other.astype(jnp.float32)).reshape(4, 4, 2, *TILE)
    code = code.transpose(2, 1, 0, 3, 4)
    return (jnp.flip(code, (0, 1, 2)) if core else code).reshape(32, *TILE)


def in_place(first, second):
    first, second = first.reshape(2, 4, 4, *TILE), jnp.flip(second.reshape(2, 4, 4, *TILE), (0, 1, 2))
    first, second = (half.transpose(2, 1, 0, 3, 4).reshape(16, 2, *TILE) for half in (first, second))
    return jnp.stack([first, second], axis=1)


def update(gradient, master, moment_one, moment_two):
    new_moment_one = 0.9 * moment_one + 0.1 * gradient
    new_moment_two = 0.95 * moment_two + 0.05 * gradient * gradient
    first_hat = new_moment_one / (1.0 - 0.9**STEP)
    second_hat = new_moment_two / (1.0 - 0.95**STEP)
    new_master = master - 0.003 * (first_hat / (jnp.sqrt(second_hat) + 1e-08) + 0.1 * master)
    return new_master, new_moment_one, new_moment_two


def on_device(grads, residual, master, moment_one, moment_two):
    core = lax.axis_index("core")
    blocks = lax.optimization_barrier(grads.reshape(16, 2, 2, *TILE))
    half = lambda blocks, which: lax.dynamic_index_in_dim(blocks, which, 1, False).astype(jnp.bfloat16)
    leaving = half(blocks, 1 - core)
    other = lax.ppermute(leaving, "core", SWAP)
    blocks, _ = lax.optimization_barrier((blocks, leaving))
    own = lax.optimization_barrier(half(blocks, core))
    zero = core == 0
    leaving = lax.cond(zero, lambda *halves: outgoing(*halves, 0), lambda *halves: outgoing(*halves, 1), own, other)
    arrived = exchange(leaving, REDUCE)
    slice_sum = jnp.sum(decoded(arrived), axis=0).reshape(-1)
    corrected = slice_sum + residual[0]
    sent = jnp.floor(corrected * 4.0 + 0.5) * 0.25
    new_residual = (corrected - sent)[None]
    narrow = sent.astype(jnp.bfloat16)
    sents = [lax.ppermute(narrow, "cuts", [(i, (i + shift) % 4) for i in range(4)]) for shift in (3, 2, 1)]
    new_residual, sents = lax.optimization_barrier((new_residual, sents))
    gradient = sent + sum(one.astype(jnp.float32) for one in sents)
    state = (gradient, master, moment_one, moment_two)
    rounded = update(*state)[0].astype(jnp.bfloat16).reshape(TILE)
    mine = exchange(jnp.broadcast_to(rounded, (32, *TILE)), GATHER)
    mine, state = lax.optimization_barrier((mine, state))
    theirs = lax.ppermute(mine, "core", SWAP)
    new_master, new_moment_one, new_moment_two = update(*state)
    params = in_place(jnp.where(zero, mine, theirs), jnp.where(zero, theirs, mine))
    return (params.reshape(-1), new_master, new_moment_one, new_moment_two, new_residual)


def solution(mesh):
    mesh = Mesh(mesh.devices.reshape(4, 4, 4, 2, 2), ("cuts",) + OWN)
    own = P(OWN)
    return jax.shard_map(
        on_device,
        mesh=mesh,
        in_specs=(P(("cuts",) + OWN, None), P("cuts", OWN), own, own, own),
        out_specs=(P(), own, own, own, P("cuts", OWN)),
        check_vma=False,
    )
```

```python
import itertools

import jax
import jax.numpy as jnp
from jax import lax
from jax.sharding import Mesh, PartitionSpec as P

STEP = 10
OWN = ("x", "y", "core", "dp")
TILE = (128, 128)
SWAP = [(0, 1), (1, 0)]
TURNS = [
    [(2 * cut + core, 2 * ((cut + (-shift if core else shift)) % 4) + core) for cut in range(4) for core in range(2)]
    for shift in (3, 2, 1)
]


def coded(total):
    inner = jnp.clip(total, -1.0, 1.0)
    return jnp.where(total == inner, total, (total - inner) * 1024.0).astype(jnp.bfloat16)


def decoded(code):
    code = code.astype(jnp.float32)
    return jnp.where(jnp.abs(code) > 2.0, code * (1.0 / 1024.0) + jnp.clip(code, -1.0, 1.0), code)


REDUCE = [(x, y, z) for z, y, x in itertools.product(range(2), range(4), range(4))]
GATHER = [(x, y, z) for z, y, x in itertools.product(range(2), range(4), range(4))]


def exchange(blocks, chips):
    groups = [
        [(((cut * 4 + x) * 4 + y) * 2 + core) * 2 + z for x, y, z in (chips[::-1] if core else chips)]
        for cut in range(4)
        for core in range(2)
    ]
    return lax.all_to_all(blocks, ("cuts",) + OWN, 0, 0, axis_index_groups=groups, tiled=True)


def outgoing(own, other, core):
    code = coded(own.astype(jnp.float32) + other.astype(jnp.float32)).reshape(4, 4, 2, *TILE)
    code = code.transpose(2, 1, 0, 3, 4)
    return (jnp.flip(code, (0, 1, 2)) if core else code).reshape(32, *TILE)


def in_place(first, second):
    first, second = first.reshape(2, 4, 4, *TILE), jnp.flip(second.reshape(2, 4, 4, *TILE), (0, 1, 2))
    first, second = (half.transpose(2, 1, 0, 3, 4).reshape(16, 2, *TILE) for half in (first, second))
    return jnp.stack([first, second], axis=1)


def update(gradient, master, moment_one, moment_two):
    new_moment_one = 0.9 * moment_one + 0.1 * gradient
    new_moment_two = 0.95 * moment_two + 0.05 * gradient * gradient
    first_hat = new_moment_one / (1.0 - 0.9**STEP)
    second_hat = new_moment_two / (1.0 - 0.95**STEP)
    new_master = master - 0.003 * (first_hat / (jnp.sqrt(second_hat) + 1e-08) + 0.1 * master)
    return new_master, new_moment_one, new_moment_two


def on_device(grads, residual, master, moment_one, moment_two):
    core = lax.axis_index("core")
    blocks = lax.optimization_barrier(grads.reshape(16, 2, 2, *TILE))
    half = lambda blocks, which: lax.dynamic_index_in_dim(blocks, which, 1, False).astype(jnp.bfloat16)
    leaving = half(blocks, 1 - core)
    other = lax.ppermute(leaving, "core", SWAP)
    blocks, _ = lax.optimization_barrier((blocks, leaving))
    own = lax.optimization_barrier(half(blocks, core))
    zero = core == 0
    leaving = lax.cond(zero, lambda *halves: outgoing(*halves, 0), lambda *halves: outgoing(*halves, 1), own, other)
    arrived = exchange(leaving, REDUCE)
    slice_sum = jnp.sum(decoded(arrived), axis=0).reshape(-1)
    corrected = slice_sum + residual[0]
    sent = jnp.floor(corrected * 4.0 + 0.5) * 0.25
    new_residual = (corrected - sent)[None]
    narrow = sent.astype(jnp.bfloat16)
    sents = [lax.ppermute(narrow, ("cuts", "core"), turn) for turn in TURNS]
    new_residual, sents = lax.optimization_barrier((new_residual, sents))
    gradient = sent + sum(one.astype(jnp.float32) for one in sents)
    state = (gradient, master, moment_one, moment_two)
    rounded = update(*state)[0].astype(jnp.bfloat16).reshape(TILE)
    mine = exchange(jnp.broadcast_to(rounded, (32, *TILE)), GATHER)
    mine, state = lax.optimization_barrier((mine, state))
    theirs = lax.ppermute(mine, "core", SWAP)
    new_master, new_moment_one, new_moment_two = update(*state)
    params = in_place(jnp.where(zero, mine, theirs), jnp.where(zero, theirs, mine))
    return (params.reshape(-1), new_master, new_moment_one, new_moment_two, new_residual)


def solution(mesh):
    mesh = Mesh(mesh.devices.reshape(4, 4, 4, 2, 2), ("cuts",) + OWN)
    own = P(OWN)
    return jax.shard_map(
        on_device,
        mesh=mesh,
        in_specs=(P(("cuts",) + OWN, None), P("cuts", OWN), own, own, own),
        out_specs=(P(), own, own, own, P("cuts", OWN)),
        check_vma=False,
    )
```

```python
import itertools

import jax
import jax.numpy as jnp
from jax import lax
from jax.sharding import Mesh, PartitionSpec as P

STEP = 10
OWN = ("x", "y", "core", "dp")
TILE = (128, 128)
SWAP = [(0, 1), (1, 0)]
TURNS = [
    [(2 * cut + core, 2 * ((cut + (-shift if core else shift)) % 4) + core) for cut in range(4) for core in range(2)]
    for shift in (2, 1, 3)
]


def coded(total):
    inner = jnp.clip(total, -1.0, 1.0)
    return jnp.where(total == inner, total, (total - inner) * 1024.0).astype(jnp.bfloat16)


def decoded(code):
    code = code.astype(jnp.float32)
    return jnp.where(jnp.abs(code) > 2.0, code * (1.0 / 1024.0) + jnp.clip(code, -1.0, 1.0), code)


REDUCE = [(x, y, z) for z, y, x in itertools.product(range(2), range(4), range(4))]
GATHER = [(x, y, z) for z, y, x in itertools.product(range(2), range(4), range(4))]


def exchange(blocks, chips):
    groups = [
        [(((cut * 4 + x) * 4 + y) * 2 + core) * 2 + z for x, y, z in (chips[::-1] if core else chips)]
        for cut in range(4)
        for core in range(2)
    ]
    return lax.all_to_all(blocks, ("cuts",) + OWN, 0, 0, axis_index_groups=groups, tiled=True)


def outgoing(own, other, core):
    code = coded(own.astype(jnp.float32) + other.astype(jnp.float32)).reshape(4, 4, 2, *TILE)
    code = code.transpose(2, 1, 0, 3, 4)
    return (jnp.flip(code, (0, 1, 2)) if core else code).reshape(32, *TILE)


def in_place(first, second):
    first, second = first.reshape(2, 4, 4, *TILE), jnp.flip(second.reshape(2, 4, 4, *TILE), (0, 1, 2))
    first, second = (half.transpose(2, 1, 0, 3, 4).reshape(16, 2, *TILE) for half in (first, second))
    return jnp.stack([first, second], axis=1)


def update(gradient, master, moment_one, moment_two):
    new_moment_one = 0.9 * moment_one + 0.1 * gradient
    new_moment_two = 0.95 * moment_two + 0.05 * gradient * gradient
    first_hat = new_moment_one / (1.0 - 0.9**STEP)
    second_hat = new_moment_two / (1.0 - 0.95**STEP)
    new_master = master - 0.003 * (first_hat / (jnp.sqrt(second_hat) + 1e-08) + 0.1 * master)
    return new_master, new_moment_one, new_moment_two


def on_device(grads, residual, master, moment_one, moment_two):
    core = lax.axis_index("core")
    blocks = lax.optimization_barrier(grads.reshape(16, 2, 2, *TILE))
    half = lambda blocks, which: lax.dynamic_index_in_dim(blocks, which, 1, False).astype(jnp.bfloat16)
    leaving = half(blocks, 1 - core)
    other = lax.ppermute(leaving, "core", SWAP)
    blocks, _ = lax.optimization_barrier((blocks, leaving))
    own = lax.optimization_barrier(half(blocks, core))
    zero = core == 0
    leaving = lax.cond(zero, lambda *halves: outgoing(*halves, 0), lambda *halves: outgoing(*halves, 1), own, other)
    arrived = exchange(leaving, REDUCE)
    slice_sum = jnp.sum(decoded(arrived), axis=0).reshape(-1)
    corrected = slice_sum + residual[0]
    sent = jnp.floor(corrected * 4.0 + 0.5) * 0.25
    new_residual = (corrected - sent)[None]
    narrow = sent.astype(jnp.bfloat16)
    sents = [lax.ppermute(narrow, ("cuts", "core"), turn) for turn in TURNS]
    new_residual, sents = lax.optimization_barrier((new_residual, sents))
    gradient = sent + sum(one.astype(jnp.float32) for one in sents)
    state = (gradient, master, moment_one, moment_two)
    rounded = update(*state)[0].astype(jnp.bfloat16).reshape(TILE)
    mine = exchange(jnp.broadcast_to(rounded, (32, *TILE)), GATHER)
    mine, state = lax.optimization_barrier((mine, state))
    theirs = lax.ppermute(mine, "core", SWAP)
    new_master, new_moment_one, new_moment_two = update(*state)
    params = in_place(jnp.where(zero, mine, theirs), jnp.where(zero, theirs, mine))
    return (params.reshape(-1), new_master, new_moment_one, new_moment_two, new_residual)


def solution(mesh):
    mesh = Mesh(mesh.devices.reshape(4, 4, 4, 2, 2), ("cuts",) + OWN)
    own = P(OWN)
    return jax.shard_map(
        on_device,
        mesh=mesh,
        in_specs=(P(("cuts",) + OWN, None), P("cuts", OWN), own, own, own),
        out_specs=(P(), own, own, own, P("cuts", OWN)),
        check_vma=False,
    )
```

```python
import itertools

import jax
import jax.numpy as jnp
from jax import lax
from jax.sharding import Mesh, PartitionSpec as P

STEP = 10
OWN = ("x", "y", "core", "dp")
TILE = (128, 128)
SWAP = [(0, 1), (1, 0)]
TURNS = [
    [(2 * cut + core, 2 * ((cut + (-shift if core else shift)) % 4) + core) for cut in range(4) for core in range(2)]
    for shift in (3, 2, 1)
]


def coded(total):
    inner = jnp.clip(total, -1.0, 1.0)
    return jnp.where(total == inner, total, (total - inner) * 1024.0).astype(jnp.bfloat16)


def decoded(code):
    code = code.astype(jnp.float32)
    return jnp.where(jnp.abs(code) > 2.0, code * (1.0 / 1024.0) + jnp.clip(code, -1.0, 1.0), code)


REDUCE = [
    (2 * x1 + (x0 ^ x1), 2 * y1 + (y0 ^ y1), z)
    for y0, z, x0, y1, x1 in itertools.product((0, 1), repeat=5)
]
GATHER = [(x, y, z) for z, x, y in itertools.product(range(2), range(4), range(4))]


def exchange(blocks, chips):
    groups = [
        [(((cut * 4 + x) * 4 + y) * 2 + core) * 2 + z for x, y, z in (chips[::-1] if core else chips)]
        for cut in range(4)
        for core in range(2)
    ]
    return lax.all_to_all(blocks, ("cuts",) + OWN, 0, 0, axis_index_groups=groups, tiled=True)


def gray(blocks, axis):
    low, high = jnp.split(blocks, 2, axis)
    return jnp.concatenate([low, jnp.flip(high, axis)], axis)


def outgoing(own, other, core):
    code = coded(own.astype(jnp.float32) + other.astype(jnp.float32)).reshape(4, 4, 2, *TILE)
    code = gray(gray(code, 0), 1).reshape(2, 2, 2, 2, 2, *TILE)
    code = code.transpose(3, 4, 1, 2, 0, 5, 6)
    return (jnp.flip(code, (0, 1, 2, 3, 4)) if core else code).reshape(32, *TILE)


def in_place(first, second):
    first, second = first.reshape(2, 4, 4, *TILE), jnp.flip(second.reshape(2, 4, 4, *TILE), (0, 1, 2))
    first, second = (half.transpose(1, 2, 0, 3, 4).reshape(16, 2, *TILE) for half in (first, second))
    return jnp.stack([first, second], axis=1)


def update(gradient, master, moment_one, moment_two):
    new_moment_one = 0.9 * moment_one + 0.1 * gradient
    new_moment_two = 0.95 * moment_two + 0.05 * gradient * gradient
    first_hat = new_moment_one / (1.0 - 0.9**STEP)
    second_hat = new_moment_two / (1.0 - 0.95**STEP)
    new_master = master - 0.003 * (first_hat / (jnp.sqrt(second_hat) + 1e-08) + 0.1 * master)
    return new_master, new_moment_one, new_moment_two


def on_device(grads, residual, master, moment_one, moment_two):
    core = lax.axis_index("core")
    blocks = lax.optimization_barrier(grads.reshape(16, 2, 2, *TILE))
    half = lambda blocks, which: lax.dynamic_index_in_dim(blocks, which, 1, False).astype(jnp.bfloat16)
    leaving = half(blocks, 1 - core)
    other = lax.ppermute(leaving, "core", SWAP)
    blocks, _ = lax.optimization_barrier((blocks, leaving))
    own = lax.optimization_barrier(half(blocks, core))
    zero = core == 0
    leaving = lax.cond(zero, lambda *halves: outgoing(*halves, 0), lambda *halves: outgoing(*halves, 1), own, other)
    arrived = exchange(leaving, REDUCE)
    slice_sum = jnp.sum(decoded(arrived), axis=0).reshape(-1)
    corrected = slice_sum + residual[0]
    sent = jnp.floor(corrected * 4.0 + 0.5) * 0.25
    new_residual = (corrected - sent)[None]
    narrow = sent.astype(jnp.bfloat16)
    sents = [lax.ppermute(narrow, ("cuts", "core"), turn) for turn in TURNS]
    new_residual, sents = lax.optimization_barrier((new_residual, sents))
    gradient = sent + sum(one.astype(jnp.float32) for one in sents)
    state = (gradient, master, moment_one, moment_two)
    rounded = update(*state)[0].astype(jnp.bfloat16).reshape(TILE)
    mine = exchange(jnp.broadcast_to(rounded, (32, *TILE)), GATHER)
    mine, state = lax.optimization_barrier((mine, state))
    theirs = lax.ppermute(mine, "core", SWAP)
    new_master, new_moment_one, new_moment_two = update(*state)
    params = in_place(jnp.where(zero, mine, theirs), jnp.where(zero, theirs, mine))
    return (params.reshape(-1), new_master, new_moment_one, new_moment_two, new_residual)


def solution(mesh):
    mesh = Mesh(mesh.devices.reshape(4, 4, 4, 2, 2), ("cuts",) + OWN)
    own = P(OWN)
    return jax.shard_map(
        on_device,
        mesh=mesh,
        in_specs=(P(("cuts",) + OWN, None), P("cuts", OWN), own, own, own),
        out_specs=(P(), own, own, own, P("cuts", OWN)),
        check_vma=False,
    )
```
